1024 devices in a mesh: seq: 128 (over y, z), head: 8 (over x, core).
Axes of the slice: x: 4, y: 8, z: 16, core: 2. Of those that a mesh axis runs over, the one named last changes fastest.
Arguments:
- queries: float32 [16384, 2048], P('seq', 'head'), may hold values from -6 to 6
- keys: float32 [16384, 2048], P('seq', 'head'), may hold values from -0.53033006 to 0.53033006
- values: float32 [16384, 2048], P('seq', 'head'), may hold values from -6 to 6
- out_grad: bfloat16 [16384, 2048], P('seq', 'head'), may hold values from -6 to 6
- w_out: bfloat16 [2048, 2048], P('head'), may hold values from -0.125 to 0.125
- ridge: float32 [16], P('head'), may hold values from 0.25 to 4
Outputs:
- grad_queries: float32 [16384, 2048], P('seq', 'head')
- grad_keys: float32 [16384, 2048], P('seq', 'head')
- grad_values: float32 [16384, 2048], P('seq', 'head')
The draws below stay inside these ranges and needn't reach their ends.
All inputs are finite; a program needn't handle non-finite values.
Results may differ from the reference program's by a relative error of at most 0.00035.
Values may be sent and summed in bfloat16 or wider, within the bound.
No kernel may reach another device: no remote copies, remote signals or barrier semaphores. Data moves between devices by JAX's collectives and lax.ppermute only.
A program may use at most 128 MiB of HBM per device.

```python
import math
import jax
import jax.numpy as jnp
from jax import lax

DK = 128
TOK_DEV = 128
ITERS = 2
HEADS = 16
D = 2048
TOKENS = 16384


def steps_of(stream_key, dims, cuts, low, top_value):
    gain, own = 1.0, jax.random.fold_in(stream_key, 6)
    for dim, parts in cuts:
        steps = jnp.exp(jax.random.uniform(jax.random.fold_in(own, dim), (parts,), jnp.float32, low / len(cuts), top_value / len(cuts)))
        gain = gain * jnp.repeat(steps, dims[dim] // parts).reshape([-1 if axis == dim else 1 for axis in range(len(dims))])
    return gain


def normal_values(key, dims, width, most, pieces=(), held_as=jnp.bfloat16):
    factor_of = steps_of(key, dims, pieces, -0.22, 0.18) if pieces else 1.0
    drawn = jax.random.normal(key, dims, jnp.float32) * width * factor_of
    return jnp.minimum(jnp.maximum(drawn, -most), most).astype(held_as)


def setup_inputs(seed: int = 0) -> dict:
    seeds = jax.random.split(jax.random.key(seed), 7)
    queries = normal_values(seeds[0], (TOKENS, D), 1.0, 6.0, ((0, 128), (1, 8)), jnp.float32)
    keys = normal_values(seeds[1], (TOKENS, D), (DK ** -0.5), 0.53033006, ((0, 128), (1, 8)), jnp.float32)
    values = normal_values(seeds[2], (TOKENS, D), 1.0, 6.0, ((0, 128), (1, 8)), jnp.float32)
    out_grad = normal_values(seeds[3], (TOKENS, D), 1.0, 6.0, ((0, 128), (1, 8)))
    w_out = normal_values(seeds[4], (D, D), D ** -0.5, 0.125, ((0, 8),))
    ridge = jnp.clip(jnp.exp(math.log(4.0) - 2.7725887 * jax.random.uniform(seeds[5], (HEADS,), jnp.float32) ** steps_of(seeds[5], (HEADS,), ((0, 8),), -0.2, 0.2)), 0.25, 4.0)
    return dict(queries=queries, keys=keys, values=values, out_grad=out_grad, w_out=w_out, ridge=ridge)


highest = lax.Precision.HIGHEST

def lower_mask(count):
    rows = lax.broadcasted_iota(jnp.int32, (count, count), 0)
    cols = lax.broadcasted_iota(jnp.int32, (count, count), 1)
    return (rows >= cols).astype(jnp.float32)

def local_out(query_heads, key_heads, value_heads, cov_before, valkey_before, ridge_heads):
    mask = lower_mask(query_heads.shape[1])

    def apply_matrix(direction):
        carried = jnp.einsum('hij,htj->hti', cov_before, direction, precision=highest)
        scores = jnp.einsum('htd,hsd->hts', direction, key_heads, precision=highest) * mask
        inner = jnp.einsum('hts,hsd->htd', scores, key_heads, precision=highest)
        return carried + inner + ridge_heads[:, None, None] * direction
    solution = jnp.zeros_like(query_heads)
    resid = query_heads
    direction = query_heads
    norm_now = lax.optimization_barrier(jnp.sum(resid * resid, axis=-1, keepdims=True))
    for step in range(ITERS):
        image = apply_matrix(direction)
        alpha = norm_now / (lax.optimization_barrier(jnp.sum(direction * image, axis=-1, keepdims=True)) + 1e-06)
        solution = solution + alpha * direction
        resid = resid - alpha * image
        norm_next = lax.optimization_barrier(jnp.sum(resid * resid, axis=-1, keepdims=True))
        direction = resid + norm_next / (norm_now + 1e-06) * direction
        norm_now = norm_next
    carried = jnp.einsum('hij,htj->hti', valkey_before, solution, precision=highest)
    scores = jnp.einsum('htd,hsd->hts', solution, key_heads, precision=highest) * mask
    return carried + jnp.einsum('hts,hsd->htd', scores, value_heads, precision=highest)

def one_head(query_rows, key_rows, value_rows, ridge_value):
    blocks = TOKENS // TOK_DEV
    query_blocks = query_rows.reshape(blocks, TOK_DEV, DK)
    key_blocks = key_rows.reshape(blocks, TOK_DEV, DK)
    value_blocks = value_rows.reshape(blocks, TOK_DEV, DK)
    cov_sums = jnp.einsum('btd,bte->bde', key_blocks, key_blocks, precision=highest)
    valkey_sums = jnp.einsum('bti,btj->bij', value_blocks, key_blocks, precision=highest)
    cov_before = jnp.cumsum(cov_sums, axis=0) - cov_sums
    valkey_before = jnp.cumsum(valkey_sums, axis=0) - valkey_sums
    ridge_blocks = jnp.zeros((blocks,), jnp.float32) + ridge_value
    result = local_out(query_blocks, key_blocks, value_blocks, cov_before, valkey_before, ridge_blocks)
    return result.reshape(TOKENS, DK)

def reference(queries, keys, values, out_grad, w_out, ridge):
    d_out = jnp.dot(out_grad, w_out.T, preferred_element_type=jnp.float32)

    def split_heads(array):
        return array.reshape(TOKENS, HEADS, DK).transpose(1, 0, 2)

    def per_head(items):
        query_rows, key_rows, value_rows, grad_rows, ridge_value = items

        def forward(query_in, key_in, value_in):
            return one_head(query_in, key_in, value_in, ridge_value)
        unused, pull = jax.vjp(forward, query_rows, key_rows, value_rows)
        return pull(grad_rows)
    grads = lax.map(per_head, (split_heads(queries), split_heads(keys), split_heads(values), split_heads(d_out), ridge))

    def join_heads(array):
        return array.transpose(1, 0, 2).reshape(TOKENS, HEADS * DK)
    return (join_heads(grads[0]), join_heads(grads[1]), join_heads(grads[2]))
```

```python
import functools

import jax
import jax.numpy as jnp
from jax import lax
from jax.experimental import pallas as pl
from jax.experimental.pallas import tpu as pltpu
from jax.sharding import PartitionSpec as P

EPS = 1e-06
F32 = jnp.float32
BF16 = jnp.bfloat16


def halves(a):
    high = a.astype(BF16)
    return high, (a - high.astype(F32)).astype(BF16)


def left(a):
    return jnp.concatenate(halves(a), axis=1)


def right(b):
    row = jnp.concatenate(halves(b), axis=1)
    return jnp.concatenate([row, row], axis=0)


def right_t(b):
    column = jnp.concatenate(halves(b), axis=0)
    return jnp.concatenate([column, column], axis=1)


def fold(wide):
    n = wide.shape[1] // 2
    return wide[:, :n] + wide[:, n:]


def mul(a2, b2):
    return fold(lax.dot_general(a2, b2, (((1,), (0,)), ((), ())), preferred_element_type=F32))


def mul_t(a2, b2):
    return fold(lax.dot_general(a2, b2, (((1,), (1,)), ((), ())), preferred_element_type=F32))


def row_dot(a, b):
    return jnp.sum(a * b, axis=-1, keepdims=True)


def column_block(ref, h, size):
    return ref[:, h * size : (h + 1) * size]


def state_kernel(k_ref, v_ref, out_ref, *, heads, size):
    for h in range(heads):
        k = column_block(k_ref, h, size)
        v = column_block(v_ref, h, size)
        key_side = right(k)
        out_ref[:, h * size : (h + 1) * size] = mul(left(k.T), key_side)
        out_ref[:, (heads + h) * size : (heads + h + 1) * size] = mul(left(v.T), key_side)


def scan_kernel(x_ref, out_ref, *, backward):
    x = x_ref[...]
    count = x.shape[0]
    rows = lax.broadcasted_iota(jnp.int32, (count, count), 0)
    cols = lax.broadcasted_iota(jnp.int32, (count, count), 1)
    earlier = ((cols > rows) if backward else (cols < rows)).astype(F32).astype(BF16)
    total = None
    rest = x
    for _ in range(3):
        piece = rest.astype(BF16)
        rest = rest - piece.astype(F32)
        part = lax.dot_general(earlier, piece, (((1,), (0,)), ((), ())), preferred_element_type=F32)
        total = part if total is None else total + part
    out_ref[...] = total


def main_kernel(
    ridge_ref, q_ref, k_ref, v_ref, do_ref, state_ref,
    gq_ref, gk_ref, gv_ref, out_ref, *, heads, size,
):
    tokens = q_ref.shape[0]
    rows = lax.broadcasted_iota(jnp.int32, (tokens, tokens), 0)
    cols = lax.broadcasted_iota(jnp.int32, (tokens, tokens), 1)
    mask = rows >= cols
    each = range(heads)

    def masked(scores):
        return jnp.where(mask, scores, 0.0)

    q = [column_block(q_ref, h, size) for h in each]
    k = [column_block(k_ref, h, size) for h in each]
    v = [column_block(v_ref, h, size) for h in each]
    do = [column_block(do_ref, h, size) for h in each]
    cov = [right(column_block(state_ref, h, size)) for h in each]
    valkey = [right(column_block(state_ref, heads + h, size)) for h in each]
    ridge = [ridge_ref[h] for h in each]
    k_plain = [right(k[h]) for h in each]
    k_turned = [right_t(k[h]) for h in each]

    def apply_matrix(p):
        p2 = [left(p[h]) for h in each]
        scores = [masked(mul_t(p2[h], k_turned[h])) for h in each]
        carried = [mul(p2[h], cov[h]) for h in each]
        image = [mul(left(scores[h]), k_plain[h]) + carried[h] + ridge[h] * p[h] for h in each]
        return scores, image

    s0, a0 = apply_matrix(q)
    do2 = [left(do[h]) for h in each]
    sw = [masked(mul_t(do2[h], right_t(v[h]))) for h in each]
    xb = [mul(left(sw[h]), k_plain[h]) + mul(do2[h], valkey[h]) for h in each]

    n0 = [row_dot(q[h], q[h]) for h in each]
    d0 = [row_dot(q[h], a0[h]) + EPS for h in each]
    al0 = [n0[h] / d0[h] for h in each]
    r1 = [q[h] - al0[h] * a0[h] for h in each]
    n1 = [row_dot(r1[h], r1[h]) for h in each]
    beta = [n1[h] / (n0[h] + EPS) for h in each]
    p1 = [r1[h] + beta[h] * q[h] for h in each]
    s1, a1 = apply_matrix(p1)
    d1 = [row_dot(p1[h], a1[h]) + EPS for h in each]
    al1 = [n1[h] / d1[h] for h in each]

    al1b = [row_dot(xb[h], p1[h]) for h in each]
    n1b = [al1b[h] / d1[h] for h in each]
    d1b = [-n1b[h] * al1[h] for h in each]
    p1b = [al1[h] * xb[h] + (2.0 * d1b[h]) * a1[h] for h in each]
    betab = [row_dot(p1b[h], q[h]) for h in each]
    n1b = [n1b[h] + betab[h] / (n0[h] + EPS) for h in each]
    n0b = [-betab[h] * beta[h] / (n0[h] + EPS) for h in each]
    r1b = [p1b[h] + (2.0 * n1b[h]) * r1[h] for h in each]
    al0b = [row_dot(xb[h], q[h]) - row_dot(r1b[h], a0[h]) for h in each]
    d0b = [-al0b[h] * al0[h] / d0[h] for h in each]
    n0b = [n0b[h] + al0b[h] / d0[h] for h in each]
    a0b = [d0b[h] * q[h] - al0[h] * r1b[h] for h in each]
    s2, back = apply_matrix(a0b)

    for h in each:
        here = slice(h * size, (h + 1) * size)
        x = al0[h] * q[h] + al1[h] * p1[h]
        sx = al0[h] * s0[h] + al1[h] * s1[h]
        c1 = (2.0 * d1b[h]) * p1[h]
        gq_ref[:, here] = (
            beta[h] * p1b[h] + al0[h] * xb[h] + d0b[h] * a0[h] + back[h] + r1b[h]
            + (2.0 * n0b[h]) * q[h]
        )
        x2, q2, p2, a2, do2_right = right(x), right(q[h]), right(p1[h]), right(a0b[h]), right(do[h])
        c2 = right(c1)
        gk_ref[:, here] = (
            mul(left(sw[h].T), x2) + mul(left(s1[h].T), c2)
            + mul(left(s0[h].T), a2) + mul(left(s2[h].T), q2)
        )
        gv_ref[:, here] = mul(left(sx.T), do2_right)
        out_ref[:, here] = (
            mul(left(c1.T), p2) + mul(left(a0b[h].T), q2) + mul(left(q[h].T), a2)
        )
        out_ref[:, (heads + h) * size : (heads + h + 1) * size] = mul(left(do[h].T), x2)


def final_kernel(k_ref, v_ref, gk_ref, gv_ref, state_ref, gk_out, gv_out, *, heads, size):
    for h in range(heads):
        here = slice(h * size, (h + 1) * size)
        cov = column_block(state_ref, h, size)
        valkey = column_block(state_ref, heads + h, size)
        k2 = left(k_ref[:, here])
        v2 = left(v_ref[:, here])
        gk_out[:, here] = gk_ref[:, here] + mul(k2, right(cov)) + mul(v2, right(valkey))
        gv_out[:, here] = gv_ref[:, here] + mul_t(k2, right_t(valkey))


VMEM = pl.BlockSpec(memory_space=pltpu.VMEM)
SMEM = pl.BlockSpec(memory_space=pltpu.SMEM)
PARAMS = pltpu.CompilerParams(vmem_limit_bytes=32 * 1024 * 1024)


def call(kernel, in_specs, out_shape):
    out_specs = VMEM if not isinstance(out_shape, tuple) else (VMEM,) * len(out_shape)
    return pl.pallas_call(
        kernel, in_specs=in_specs, out_specs=out_specs, out_shape=out_shape, compiler_params=PARAMS
    )


def scan_over(state, backward):
    count = lax.axis_size("seq")
    width = state.shape[0] * state.shape[1] // count
    parts = lax.all_to_all(state.reshape(count, width), "seq", 0, 0, tiled=True)
    sums = call(
        functools.partial(scan_kernel, backward=backward),
        [VMEM],
        jax.ShapeDtypeStruct(parts.shape, F32),
    )(parts)
    return lax.all_to_all(sums, "seq", 0, 0, tiled=True).reshape(state.shape)


def on_device(queries, keys, values, out_grad, w_out, ridge):
    tokens, columns = queries.shape
    heads = ridge.shape[0]
    size = columns // heads
    sizes = dict(heads=heads, size=size)
    local = jax.ShapeDtypeStruct((tokens, columns), F32)
    state_shape = jax.ShapeDtypeStruct((size, 2 * columns), F32)

    states = call(functools.partial(state_kernel, **sizes), [VMEM] * 2, state_shape)(keys, values)
    before = scan_over(states, False)
    d_out = lax.dot_general(
        lax.all_gather(out_grad, "head", axis=1, tiled=True),
        w_out,
        (((1,), (1,)), ((), ())),
        preferred_element_type=F32,
    )
    grad_q, grad_k, grad_v, adjoints = call(
        functools.partial(main_kernel, **sizes),
        [SMEM] + [VMEM] * 5,
        (local, local, local, state_shape),
    )(ridge, queries, keys, values, d_out, before)
    later = scan_over(adjoints, True)
    grad_k, grad_v = call(
        functools.partial(final_kernel, **sizes), [VMEM] * 5, (local, local)
    )(keys, values, grad_k, grad_v, later)
    return grad_q, grad_k, grad_v


def solution(mesh):
    rows = P("seq", "head")
    return jax.shard_map(
        on_device,
        mesh=mesh,
        in_specs=(rows, rows, rows, rows, P("head", None), P("head")),
        out_specs=(rows, rows, rows),
        check_vma=False,
    )
```

```python
import functools

import jax
import jax.numpy as jnp
from jax import lax
from jax.experimental import pallas as pl
from jax.experimental.pallas import tpu as pltpu
from jax.sharding import PartitionSpec as P

EPS = 1e-06
F32 = jnp.float32
BF16 = jnp.bfloat16


def halves(a):
    high = a.astype(BF16)
    return high, (a - high.astype(F32)).astype(BF16)


def left(a):
    return jnp.concatenate(halves(a), axis=1)


def right(b):
    row = jnp.concatenate(halves(b), axis=1)
    return jnp.concatenate([row, row], axis=0)


def right_t(b):
    column = jnp.concatenate(halves(b), axis=0)
    return jnp.concatenate([column, column], axis=1)


def fold(wide):
    n = wide.shape[1] // 2
    return wide[:, :n] + wide[:, n:]


def mul(a2, b2):
    return fold(lax.dot_general(a2, b2, (((1,), (0,)), ((), ())), preferred_element_type=F32))


def mul_t(a2, b2):
    return fold(lax.dot_general(a2, b2, (((1,), (1,)), ((), ())), preferred_element_type=F32))


def row_dot(a, b):
    return jnp.sum(a * b, axis=-1, keepdims=True)


def column_block(ref, h, size):
    return ref[:, h * size : (h + 1) * size]


def square_iota(size):
    rows = lax.broadcasted_iota(jnp.int32, (size, size), 0)
    return rows, lax.broadcasted_iota(jnp.int32, (size, size), 1)


def pack(cov, valkey, out_ref):
    parts, size = out_ref.shape[0], cov[0].shape[0]
    each = size // parts
    rows, cols = square_iota(size)
    both = jnp.where(rows <= cols, cov[0], cov[1])
    for i, matrix in enumerate((both, *valkey)):
        for r in range(each):
            at = (i * each + r) * size
            out_ref[:, at : at + size] = matrix[r * parts : (r + 1) * parts]
    diagonal = jnp.sum(jnp.where(rows == cols, cov[1], 0.0), axis=0, keepdims=True)
    owner = lax.broadcasted_iota(jnp.int32, (parts, size), 0)
    lane = lax.broadcasted_iota(jnp.int32, (parts, size), 1)
    mine = (lane >= owner * each) & (lane < (owner + 1) * each)
    out_ref[:, 3 * each * size :] = jnp.where(mine, diagonal, 0.0)


def unpack(ref, size):
    parts = ref.shape[0]
    each = size // parts

    def matrix(i):
        pieces = [ref[:, at * size : (at + 1) * size] for at in range(i * each, (i + 1) * each)]
        return jnp.concatenate(pieces, axis=0)

    both = matrix(0)
    turned = both.T
    rows, cols = square_iota(size)
    diagonal = jnp.sum(ref[:, 3 * each * size :], axis=0, keepdims=True)
    first = jnp.where(rows <= cols, both, turned)
    second = jnp.where(rows > cols, both, jnp.where(rows == cols, diagonal, turned))
    return (first, second), (matrix(1), matrix(2))


def state_kernel(k_ref, v_ref, out_ref, *, heads, size):
    cov, valkey = [], []
    for h in range(heads):
        k = column_block(k_ref, h, size)
        v = column_block(v_ref, h, size)
        key_side = right(k)
        cov.append(mul(left(k.T), key_side))
        valkey.append(mul(left(v.T), key_side))
    pack(cov, valkey, out_ref)


def inner_kernel(group_ref, x_ref, sums_ref, total_ref, *, backward):
    x = x_ref[...]
    rows, cols = square_iota(x.shape[0])
    earlier = ((cols > rows) if backward else (cols < rows)).astype(F32).astype(BF16)
    total = None
    rest = x
    for _ in range(3):
        piece = rest.astype(BF16)
        rest = rest - piece.astype(F32)
        part = lax.dot_general(earlier, piece, (((1,), (0,)), ((), ())), preferred_element_type=F32)
        total = part if total is None else total + part
    sums_ref[...] = total
    group = group_ref[0]
    reader = lax.broadcasted_iota(jnp.int32, total_ref.shape, 0)
    reads = (reader < group) if backward else (reader > group)
    total_ref[...] = jnp.where(reads, jnp.sum(x, axis=0, keepdims=True), 0.0)


def outer_kernel(sums_ref, totals_ref, out_ref):
    out_ref[...] = sums_ref[...] + jnp.sum(totals_ref[...], axis=0, keepdims=True)


def main_kernel(
    ridge_ref, q_ref, k_ref, v_ref, do_ref, state_ref,
    gq_ref, gk_ref, gv_ref, out_ref, *, heads, size,
):
    tokens = q_ref.shape[0]
    rows = lax.broadcasted_iota(jnp.int32, (tokens, tokens), 0)
    cols = lax.broadcasted_iota(jnp.int32, (tokens, tokens), 1)
    mask = rows >= cols
    each = range(heads)

    def masked(scores):
        return jnp.where(mask, scores, 0.0)

    q = [column_block(q_ref, h, size) for h in each]
    k = [column_block(k_ref, h, size) for h in each]
    v = [column_block(v_ref, h, size) for h in each]
    do = [column_block(do_ref, h, size) for h in each]
    cov, valkey = [[right(m) for m in pair] for pair in unpack(state_ref, size)]
    ridge = [column_block(ridge_ref, h, size) for h in each]
    k_plain = [right(k[h]) for h in each]
    k_turned = [right_t(k[h]) for h in each]

    def apply_matrix(p):
        p2 = [left(p[h]) for h in each]
        scores = [masked(mul_t(p2[h], k_turned[h])) for h in each]
        carried = [mul(p2[h], cov[h]) for h in each]
        image = [mul(left(scores[h]), k_plain[h]) + carried[h] + ridge[h] * p[h] for h in each]
        return scores, image

    s0, a0 = apply_matrix(q)
    do2 = [left(do[h]) for h in each]
    sw = [masked(mul_t(do2[h], right_t(v[h]))) for h in each]
    xb = [mul(left(sw[h]), k_plain[h]) + mul(do2[h], valkey[h]) for h in each]

    n0 = [row_dot(q[h], q[h]) for h in each]
    d0 = [row_dot(q[h], a0[h]) + EPS for h in each]
    al0 = [n0[h] / d0[h] for h in each]
    r1 = [q[h] - al0[h] * a0[h] for h in each]
    n1 = [row_dot(r1[h], r1[h]) for h in each]
    beta = [n1[h] / (n0[h] + EPS) for h in each]
    p1 = [r1[h] + beta[h] * q[h] for h in each]
    s1, a1 = apply_matrix(p1)
    d1 = [row_dot(p1[h], a1[h]) + EPS for h in each]
    al1 = [n1[h] / d1[h] for h in each]

    al1b = [row_dot(xb[h], p1[h]) for h in each]
    n1b = [al1b[h] / d1[h] for h in each]
    d1b = [-n1b[h] * al1[h] for h in each]
    p1b = [al1[h] * xb[h] + (2.0 * d1b[h]) * a1[h] for h in each]
    betab = [row_dot(p1b[h], q[h]) for h in each]
    n1b = [n1b[h] + betab[h] / (n0[h] + EPS) for h in each]
    n0b = [-betab[h] * beta[h] / (n0[h] + EPS) for h in each]
    r1b = [p1b[h] + (2.0 * n1b[h]) * r1[h] for h in each]
    al0b = [row_dot(xb[h], q[h]) - row_dot(r1b[h], a0[h]) for h in each]
    d0b = [-al0b[h] * al0[h] / d0[h] for h in each]
    n0b = [n0b[h] + al0b[h] / d0[h] for h in each]
    a0b = [d0b[h] * q[h] - al0[h] * r1b[h] for h in each]
    s2, back = apply_matrix(a0b)

    cov_out, valkey_out = [], []
    for h in each:
        here = slice(h * size, (h + 1) * size)
        x = al0[h] * q[h] + al1[h] * p1[h]
        sx = al0[h] * s0[h] + al1[h] * s1[h]
        c1 = (2.0 * d1b[h]) * p1[h]
        gq_ref[:, here] = (
            beta[h] * p1b[h] + al0[h] * xb[h] + d0b[h] * a0[h] + back[h] + r1b[h]
            + (2.0 * n0b[h]) * q[h]
        )
        x2, q2, p2, a2, do2_right = right(x), right(q[h]), right(p1[h]), right(a0b[h]), right(do[h])
        c2 = right(c1)
        gk_ref[:, here] = (
            mul(left(sw[h].T), x2) + mul(left(s1[h].T), c2)
            + mul(left(s0[h].T), a2) + mul(left(s2[h].T), q2)
        )
        gv_ref[:, here] = mul(left(sx.T), do2_right)
        turned = mul(left(a0b[h].T), q2)
        cov_out.append(mul(left(c1.T), p2) + turned + turned.T)
        valkey_out.append(mul(left(do[h].T), x2))
    pack(cov_out, valkey_out, out_ref)


def final_kernel(k_ref, v_ref, gk_ref, gv_ref, state_ref, gk_out, gv_out, *, heads, size):
    cov, valkey = unpack(state_ref, size)
    for h in range(heads):
        here = slice(h * size, (h + 1) * size)
        k2 = left(k_ref[:, here])
        v2 = left(v_ref[:, here])
        gk_out[:, here] = gk_ref[:, here] + mul(k2, right(cov[h])) + mul(v2, right(valkey[h]))
        gv_out[:, here] = gv_ref[:, here] + mul_t(k2, right_t(valkey[h]))


VMEM = pl.BlockSpec(memory_space=pltpu.VMEM)
SMEM = pl.BlockSpec(memory_space=pltpu.SMEM)
PARAMS = pltpu.CompilerParams(vmem_limit_bytes=32 * 1024 * 1024)


def call(kernel, in_specs, out_shape):
    out_specs = VMEM if not isinstance(out_shape, tuple) else (VMEM,) * len(out_shape)
    return pl.pallas_call(
        kernel, in_specs=in_specs, out_specs=out_specs, out_shape=out_shape, compiler_params=PARAMS
    )


def split_blocks(count):
    inner = 16 if count % 16 == 0 and count > 16 else max(1, count // 4)
    return inner, count // inner


def scan_over(state, backward, beside):
    inner, groups = split_blocks(lax.axis_size("seq"))
    within = [[g * inner + i for i in range(inner)] for g in range(groups)]
    across = [[g * inner + i for g in range(groups)] for i in range(inner)]

    def exchange(array, members):
        return lax.all_to_all(array, "seq", 0, 0, axis_index_groups=members, tiled=True)

    received, beside = lax.optimization_barrier((exchange(state, within), beside))
    same = jax.ShapeDtypeStruct(state.shape, F32)
    sums, totals = call(
        functools.partial(inner_kernel, backward=backward),
        [SMEM, VMEM],
        (same, jax.ShapeDtypeStruct((groups, state.shape[1]), F32)),
    )(beside[0], received)
    result = call(outer_kernel, [VMEM, VMEM], same)(sums, exchange(totals, across))
    return exchange(result, within), beside


def on_device(queries, keys, values, out_grad, w_out, ridge):
    tokens, columns = queries.shape
    heads = ridge.shape[0]
    size = columns // heads
    sizes = dict(heads=heads, size=size)
    local = jax.ShapeDtypeStruct((tokens, columns), F32)
    parts = split_blocks(lax.axis_size("seq"))[0]
    state_shape = jax.ShapeDtypeStruct((parts, (3 * size // parts + 1) * size), F32)

    states = call(functools.partial(state_kernel, **sizes), [VMEM] * 2, state_shape)(keys, values)
    d_out = lax.dot_general(
        lax.all_gather(out_grad, "head", axis=1, tiled=True),
        w_out,
        (((1,), (1,)), ((), ())),
        preferred_element_type=F32,
    )
    group = (lax.axis_index("seq") // split_blocks(lax.axis_size("seq"))[0]).astype(jnp.int32)
    ridge_row = jnp.repeat(ridge, size)[None]
    before, (group, d_out, ridge_row) = scan_over(
        states, False, (group.reshape(1), d_out, ridge_row)
    )
    grad_q, grad_k, grad_v, adjoints = call(
        functools.partial(main_kernel, **sizes),
        [VMEM] * 6,
        (local, local, local, state_shape),
    )(ridge_row, queries, keys, values, d_out, before)
    later, _ = scan_over(adjoints, True, (group,))
    grad_k, grad_v = call(
        functools.partial(final_kernel, **sizes), [VMEM] * 5, (local, local)
    )(keys, values, grad_k, grad_v, later)
    return grad_q, grad_k, grad_v


def solution(mesh):
    rows = P("seq", "head")
    return jax.shard_map(
        on_device,
        mesh=mesh,
        in_specs=(rows, rows, rows, rows, P("head", None), P("head")),
        out_specs=(rows, rows, rows),
        check_vma=False,
    )
```

```python
import functools

import jax
import jax.numpy as jnp
from jax import lax
from jax.experimental import pallas as pl
from jax.experimental.pallas import tpu as pltpu
from jax.sharding import PartitionSpec as P

EPS = 1e-06
F32 = jnp.float32
BF16 = jnp.bfloat16


def halves(a):
    high = a.astype(BF16)
    return high, (a - high.astype(F32)).astype(BF16)


def left(a):
    return jnp.concatenate(halves(a), axis=1)


def right(b):
    row = jnp.concatenate(halves(b), axis=1)
    return jnp.concatenate([row, row], axis=0)


def right_t(b):
    column = jnp.concatenate(halves(b), axis=0)
    return jnp.concatenate([column, column], axis=1)


def fold(wide):
    n = wide.shape[1] // 2
    return wide[:, :n] + wide[:, n:]


def mul(a2, b2):
    return fold(lax.dot_general(a2, b2, (((1,), (0,)), ((), ())), preferred_element_type=F32))


def mul_t(a2, b2):
    return fold(lax.dot_general(a2, b2, (((1,), (1,)), ((), ())), preferred_element_type=F32))


def row_dot(a, b):
    return jnp.sum(a * b, axis=-1, keepdims=True)


def column_block(ref, h, size):
    return ref[:, h * size : (h + 1) * size]


def square_iota(size):
    rows = lax.broadcasted_iota(jnp.int32, (size, size), 0)
    return rows, lax.broadcasted_iota(jnp.int32, (size, size), 1)


def put(ref, at, block):
    columns = slice(at, at + block.shape[1])
    if len(ref.shape) == 3:
        ref[:, 0, columns] = block
    else:
        ref[:, columns] = block


def pack(cov, valkey, out_ref):
    parts, size = out_ref.shape[0], cov[0].shape[0]
    each = size // parts
    rows, cols = square_iota(size)
    both = jnp.where(rows <= cols, cov[0], cov[1])
    for i, matrix in enumerate((both, *valkey)):
        for r in range(each):
            put(out_ref, (i * each + r) * size, matrix[r * parts : (r + 1) * parts])
    diagonal = jnp.sum(jnp.where(rows == cols, cov[1], 0.0), axis=0, keepdims=True)
    owner = lax.broadcasted_iota(jnp.int32, (parts, size), 0)
    lane = lax.broadcasted_iota(jnp.int32, (parts, size), 1)
    mine = (lane >= owner * each) & (lane < (owner + 1) * each)
    put(out_ref, 3 * each * size, jnp.where(mine, diagonal, 0.0))


def unpack(ref, size):
    parts = ref.shape[0]
    each = size // parts

    def matrix(i):
        pieces = [ref[:, at * size : (at + 1) * size] for at in range(i * each, (i + 1) * each)]
        return jnp.concatenate(pieces, axis=0)

    both = matrix(0)
    turned = both.T
    rows, cols = square_iota(size)
    diagonal = jnp.sum(ref[:, 3 * each * size :], axis=0, keepdims=True)
    first = jnp.where(rows <= cols, both, turned)
    second = jnp.where(rows > cols, both, jnp.where(rows == cols, diagonal, turned))
    return (first, second), (matrix(1), matrix(2))


def state_kernel(k_ref, v_ref, out_ref, *, heads, size):
    cov, valkey = [], []
    for h in range(heads):
        k = column_block(k_ref, h, size)
        v = column_block(v_ref, h, size)
        key_side = right(k)
        cov.append(mul(left(k.T), key_side))
        valkey.append(mul(left(v.T), key_side))
    pack(cov, valkey, out_ref)


def inner_kernel(group_ref, x_ref, sums_ref, total_ref, *, backward):
    x = x_ref[...]
    rows, cols = square_iota(x.shape[0])
    earlier = ((cols > rows) if backward else (cols < rows)).astype(F32).astype(BF16)
    total = None
    rest = x
    for _ in range(3):
        piece = rest.astype(BF16)
        rest = rest - piece.astype(F32)
        part = lax.dot_general(earlier, piece, (((1,), (0,)), ((), ())), preferred_element_type=F32)
        total = part if total is None else total + part
    sums_ref[...] = total
    group = group_ref[0]
    reader = lax.broadcasted_iota(jnp.int32, total_ref.shape, 0)
    reads = (reader < group) if backward else (reader > group)
    total_ref[...] = jnp.where(reads, jnp.sum(x, axis=0, keepdims=True), 0.0)


def outer_kernel(sums_ref, totals_ref, out_ref):
    out_ref[...] = sums_ref[...] + jnp.sum(totals_ref[...], axis=0, keepdims=True)


def causal(scores):
    rows, cols = square_iota(scores.shape[0])
    return jnp.where(rows >= cols, scores, 0.0)


def local_kernel(
    ridge_ref, q_ref, k_ref, v_ref, do_ref,
    q_out, s0_ref, a0_ref, sw_ref, xb_ref, plain_ref, turned_ref, *, heads, size,
):
    q_out[...] = q_ref[...]
    for h in range(heads):
        here = slice(h * size, (h + 1) * size)
        q, k = q_ref[:, here], k_ref[:, here]
        plain, turned = right(k), right_t(k)
        plain_ref[h], turned_ref[h] = plain, turned
        s0 = causal(mul_t(left(q), turned))
        sw = causal(mul_t(left(do_ref[:, here]), right_t(v_ref[:, here])))
        s0_ref[:, here], sw_ref[:, here] = s0, sw
        a0_ref[:, here] = mul(left(s0), plain) + ridge_ref[:, here] * q
        xb_ref[:, here] = mul(left(sw), plain)


def main_kernel(
    ridge_ref, do_ref, q_ref, s0_ref, a0_ref, sw_ref, xb_ref, plain_ref, turned_ref, state_ref,
    gq_ref, gk_ref, gv_ref, out_ref, *, heads, size,
):
    each = range(heads)
    ridge, do, q, s0, sw = (
        [column_block(ref, h, size) for h in each]
        for ref in (ridge_ref, do_ref, q_ref, s0_ref, sw_ref)
    )
    cov, valkey = [[right(m) for m in pair] for pair in unpack(state_ref, size)]

    def apply_matrix(p):
        p2 = [left(p[h]) for h in each]
        scores = [causal(mul_t(p2[h], turned_ref[h])) for h in each]
        carried = [mul(p2[h], cov[h]) for h in each]
        image = [mul(left(scores[h]), plain_ref[h]) + carried[h] + ridge[h] * p[h] for h in each]
        return scores, image

    a0 = [column_block(a0_ref, h, size) + mul(left(q[h]), cov[h]) for h in each]
    xb = [column_block(xb_ref, h, size) + mul(left(do[h]), valkey[h]) for h in each]

    n0 = [row_dot(q[h], q[h]) for h in each]
    d0 = [row_dot(q[h], a0[h]) + EPS for h in each]
    al0 = [n0[h] / d0[h] for h in each]
    r1 = [q[h] - al0[h] * a0[h] for h in each]
    n1 = [row_dot(r1[h], r1[h]) for h in each]
    beta = [n1[h] / (n0[h] + EPS) for h in each]
    p1 = [r1[h] + beta[h] * q[h] for h in each]
    s1, a1 = apply_matrix(p1)
    d1 = [row_dot(p1[h], a1[h]) + EPS for h in each]
    al1 = [n1[h] / d1[h] for h in each]

    al1b = [row_dot(xb[h], p1[h]) for h in each]
    n1b = [al1b[h] / d1[h] for h in each]
    d1b = [-n1b[h] * al1[h] for h in each]
    p1b = [al1[h] * xb[h] + (2.0 * d1b[h]) * a1[h] for h in each]
    betab = [row_dot(p1b[h], q[h]) for h in each]
    n1b = [n1b[h] + betab[h] / (n0[h] + EPS) for h in each]
    n0b = [-betab[h] * beta[h] / (n0[h] + EPS) for h in each]
    r1b = [p1b[h] + (2.0 * n1b[h]) * r1[h] for h in each]
    al0b = [row_dot(xb[h], q[h]) - row_dot(r1b[h], a0[h]) for h in each]
    d0b = [-al0b[h] * al0[h] / d0[h] for h in each]
    n0b = [n0b[h] + al0b[h] / d0[h] for h in each]
    a0b = [d0b[h] * q[h] - al0[h] * r1b[h] for h in each]
    s2, back = apply_matrix(a0b)

    cov_out, valkey_out = [], []
    for h in each:
        here = slice(h * size, (h + 1) * size)
        x = al0[h] * q[h] + al1[h] * p1[h]
        sx = al0[h] * s0[h] + al1[h] * s1[h]
        c1 = (2.0 * d1b[h]) * p1[h]
        gq_ref[:, here] = (
            beta[h] * p1b[h] + al0[h] * xb[h] + d0b[h] * a0[h] + back[h] + r1b[h]
            + (2.0 * n0b[h]) * q[h]
        )
        x2, q2, p2, a2, do2_right = right(x), right(q[h]), right(p1[h]), right(a0b[h]), right(do[h])
        c2 = right(c1)
        gk_ref[:, here] = (
            mul(left(sw[h].T), x2) + mul(left(s1[h].T), c2)
            + mul(left(s0[h].T), a2) + mul(left(s2[h].T), q2)
        )
        gv_ref[:, here] = mul(left(sx.T), do2_right)
        turned = mul(left(a0b[h].T), q2)
        cov_out.append(mul(left(c1.T), p2) + turned + turned.T)
        valkey_out.append(mul(left(do[h].T), x2))
    pack(cov_out, valkey_out, out_ref)


def final_kernel(k_ref, v_ref, gk_ref, gv_ref, state_ref, gk_out, gv_out, *, heads, size):
    cov, valkey = unpack(state_ref, size)
    for h in range(heads):
        here = slice(h * size, (h + 1) * size)
        k2 = left(k_ref[:, here])
        v2 = left(v_ref[:, here])
        gk_out[:, here] = gk_ref[:, here] + mul(k2, right(cov[h])) + mul(v2, right(valkey[h]))
        gv_out[:, here] = gv_ref[:, here] + mul_t(k2, right_t(valkey[h]))


VMEM = pl.BlockSpec(memory_space=pltpu.VMEM)
SMEM = pl.BlockSpec(memory_space=pltpu.SMEM)
MIB = 1024 * 1024


def call(kernel, in_specs, out_shape, limit=32):
    out_specs = VMEM if not isinstance(out_shape, tuple) else (VMEM,) * len(out_shape)
    return pl.pallas_call(
        kernel, in_specs=in_specs, out_specs=out_specs, out_shape=out_shape,
        compiler_params=pltpu.CompilerParams(vmem_limit_bytes=limit * MIB),
    )


def split_blocks(count):
    inner = 16 if count % 16 == 0 and count > 16 else max(1, count // 4)
    return inner, count // inner


def scan_over(state, backward, beside):
    inner, groups = split_blocks(lax.axis_size("seq"))
    within = [[g * inner + i for i in range(inner)] for g in range(groups)]
    across = [[g * inner + i for g in range(groups)] for i in range(inner)]

    def exchange(array, members):
        return lax.all_to_all(array, "seq", 0, 0, axis_index_groups=members, tiled=True)

    received, beside = lax.optimization_barrier((exchange(state, within), beside))
    received = received.reshape(inner, -1)
    same = jax.ShapeDtypeStruct(received.shape, F32)
    sums, totals = call(
        functools.partial(inner_kernel, backward=backward),
        [SMEM, VMEM],
        (same, jax.ShapeDtypeStruct((groups, received.shape[1]), F32)),
    )(beside[0], received)
    result = call(outer_kernel, [VMEM, VMEM], same)(sums, exchange(totals, across))
    return exchange(result, within), beside


def on_device(queries, keys, values, out_grad, w_out, ridge):
    tokens, columns = queries.shape
    heads = ridge.shape[0]
    size = columns // heads
    sizes = dict(heads=heads, size=size)
    local = jax.ShapeDtypeStruct((tokens, columns), F32)
    parts = split_blocks(lax.axis_size("seq"))[0]
    state_shape = jax.ShapeDtypeStruct((parts, (3 * size // parts + 1) * size), F32)

    states_shape = jax.ShapeDtypeStruct((parts, 1, state_shape.shape[1]), F32)
    states = call(functools.partial(state_kernel, **sizes), [VMEM] * 2, states_shape, 60)(keys, values)
    d_out = lax.dot_general(
        lax.all_gather(out_grad, "head", axis=1, tiled=True),
        w_out,
        (((1,), (1,)), ((), ())),
        preferred_element_type=F32,
    )
    group = (lax.axis_index("seq") // split_blocks(lax.axis_size("seq"))[0]).astype(jnp.int32)
    ridge_row = jnp.repeat(ridge, size)[None]
    halved = jax.ShapeDtypeStruct((heads, 2 * size, 2 * size), BF16)
    here = call(
        functools.partial(local_kernel, **sizes), [VMEM] * 5, (local,) * 5 + (halved,) * 2
    )(ridge_row, queries, keys, values, d_out)
    before, (group, ridge_row, d_out, *here) = scan_over(
        states, False, (group.reshape(1), ridge_row, d_out, *here)
    )
    grad_q, grad_k, grad_v, adjoints = call(
        functools.partial(main_kernel, **sizes), [VMEM] * 10, (local, local, local, state_shape)
    )(ridge_row, d_out, *here, before)
    later, _ = scan_over(adjoints, True, (group,))
    grad_k, grad_v = call(
        functools.partial(final_kernel, **sizes), [VMEM] * 5, (local, local)
    )(keys, values, grad_k, grad_v, later)
    return grad_q, grad_k, grad_v


def solution(mesh):
    rows = P("seq", "head")
    return jax.shard_map(
        on_device,
        mesh=mesh,
        in_specs=(rows, rows, rows, rows, P("head", None), P("head")),
        out_specs=(rows, rows, rows),
        check_vma=False,
    )
```

```python
import functools

import jax
import jax.numpy as jnp
from jax import lax
from jax.experimental import pallas as pl
from jax.experimental.pallas import tpu as pltpu
from jax.sharding import PartitionSpec as P

EPS = 1e-06
F32 = jnp.float32
BF16 = jnp.bfloat16


def halves(a):
    high = a.astype(BF16)
    return high, (a - high.astype(F32)).astype(BF16)


def left(a):
    return jnp.concatenate(halves(a), axis=1)


def right(b):
    row = jnp.concatenate(halves(b), axis=1)
    return jnp.concatenate([row, row], axis=0)


def right_t(b):
    column = jnp.concatenate(halves(b), axis=0)
    return jnp.concatenate([column, column], axis=1)


def fold(wide):
    n = wide.shape[1] // 2
    return wide[:, :n] + wide[:, n:]


def mul(a2, b2):
    return fold(lax.dot_general(a2, b2, (((1,), (0,)), ((), ())), preferred_element_type=F32))


def mul_t(a2, b2):
    return fold(lax.dot_general(a2, b2, (((1,), (1,)), ((), ())), preferred_element_type=F32))


def row_dot(a, b):
    return jnp.sum(a * b, axis=-1, keepdims=True)


def column_block(ref, h, size):
    return ref[:, h * size : (h + 1) * size]


def square_iota(size):
    rows = lax.broadcasted_iota(jnp.int32, (size, size), 0)
    return rows, lax.broadcasted_iota(jnp.int32, (size, size), 1)


def put(ref, at, block):
    columns = slice(at, at + block.shape[1])
    if len(ref.shape) == 3:
        ref[:, 0, columns] = block
    else:
        ref[:, columns] = block


def pack(cov, valkey, out_ref):
    parts, size = out_ref.shape[0], cov[0].shape[0]
    each = size // parts
    rows, cols = square_iota(size)
    both = jnp.where(rows <= cols, cov[0], cov[1])
    for i, matrix in enumerate((both, *valkey)):
        for r in range(each):
            put(out_ref, (i * each + r) * size, matrix[r * parts : (r + 1) * parts])
    diagonal = jnp.sum(jnp.where(rows == cols, cov[1], 0.0), axis=0, keepdims=True)
    owner = lax.broadcasted_iota(jnp.int32, (parts, size), 0)
    lane = lax.broadcasted_iota(jnp.int32, (parts, size), 1)
    mine = (lane >= owner * each) & (lane < (owner + 1) * each)
    put(out_ref, 3 * each * size, jnp.where(mine, diagonal, 0.0))


def unpack(ref, size):
    parts = ref.shape[0]
    each = size // parts

    def matrix(i):
        pieces = [ref[:, at * size : (at + 1) * size] for at in range(i * each, (i + 1) * each)]
        return jnp.concatenate(pieces, axis=0)

    both = matrix(0)
    turned = both.T
    rows, cols = square_iota(size)
    diagonal = jnp.sum(ref[:, 3 * each * size :], axis=0, keepdims=True)
    first = jnp.where(rows <= cols, both, turned)
    second = jnp.where(rows > cols, both, jnp.where(rows == cols, diagonal, turned))
    return (first, second), (matrix(1), matrix(2))


def state_kernel(k_ref, v_ref, out_ref, *, heads, size):
    cov, valkey = [], []
    for h in range(heads):
        k = column_block(k_ref, h, size)
        v = column_block(v_ref, h, size)
        key_side = right(k)
        cov.append(mul(left(k.T), key_side))
        valkey.append(mul(left(v.T), key_side))
    pack(cov, valkey, out_ref)


def inner_kernel(group_ref, x_ref, sums_ref, total_ref, *, backward):
    x = x_ref[...]
    rows, cols = square_iota(x.shape[0])
    earlier = ((cols > rows) if backward else (cols < rows)).astype(F32).astype(BF16)
    total = None
    rest = x
    for _ in range(3):
        piece = rest.astype(BF16)
        rest = rest - piece.astype(F32)
        part = lax.dot_general(earlier, piece, (((1,), (0,)), ((), ())), preferred_element_type=F32)
        total = part if total is None else total + part
    sums_ref[...] = total
    group = group_ref[0]
    reader = lax.broadcasted_iota(jnp.int32, total_ref.shape, 0)
    reads = (reader < group) if backward else (reader > group)
    total_ref[...] = jnp.where(reads, jnp.sum(x, axis=0, keepdims=True), 0.0)


def outer_kernel(sums_ref, totals_ref, out_ref):
    out_ref[...] = sums_ref[...] + jnp.sum(totals_ref[...], axis=0, keepdims=True)


def causal(scores):
    rows, cols = square_iota(scores.shape[0])
    return jnp.where(rows >= cols, scores, 0.0)


def query_kernel(
    q_ref, k_ref, v_ref, q_out, s0_ref, a0_ref, plain_ref, turned_ref, values_ref, *, heads, size
):
    q_out[...] = q_ref[...]
    for h in range(heads):
        here = slice(h * size, (h + 1) * size)
        q, k = q_ref[:, here], k_ref[:, here]
        plain, turned = right(k), right_t(k)
        plain_ref[h], turned_ref[h], values_ref[h] = plain, turned, right_t(v_ref[:, here])
        s0 = causal(mul_t(left(q), turned))
        s0_ref[:, here] = s0
        a0_ref[:, here] = mul(left(s0), plain)


def cotangent_kernel(do_ref, plain_ref, values_ref, sw_ref, xb_ref, *, heads, size):
    for h in range(heads):
        here = slice(h * size, (h + 1) * size)
        sw = causal(mul_t(left(do_ref[:, here]), values_ref[h]))
        sw_ref[:, here] = sw
        xb_ref[:, here] = mul(left(sw), plain_ref[h])


def main_kernel(
    ridge_ref, do_ref, q_ref, s0_ref, a0_ref, plain_ref, turned_ref, sw_ref, xb_ref, state_ref,
    gq_ref, gk_ref, gv_ref, out_ref, *, heads, size,
):
    each = range(heads)
    ridge, do, q, s0, sw = (
        [column_block(ref, h, size) for h in each]
        for ref in (ridge_ref, do_ref, q_ref, s0_ref, sw_ref)
    )
    cov, valkey = [[right(m) for m in pair] for pair in unpack(state_ref, size)]

    def apply_matrix(p):
        p2 = [left(p[h]) for h in each]
        scores = [causal(mul_t(p2[h], turned_ref[h])) for h in each]
        carried = [mul(p2[h], cov[h]) for h in each]
        image = [mul(left(scores[h]), plain_ref[h]) + carried[h] + ridge[h] * p[h] for h in each]
        return scores, image

    a0 = [
        column_block(a0_ref, h, size) + ridge[h] * q[h] + mul(left(q[h]), cov[h]) for h in each
    ]
    xb = [column_block(xb_ref, h, size) + mul(left(do[h]), valkey[h]) for h in each]

    n0 = [row_dot(q[h], q[h]) for h in each]
    d0 = [row_dot(q[h], a0[h]) + EPS for h in each]
    al0 = [n0[h] / d0[h] for h in each]
    r1 = [q[h] - al0[h] * a0[h] for h in each]
    n1 = [row_dot(r1[h], r1[h]) for h in each]
    beta = [n1[h] / (n0[h] + EPS) for h in each]
    p1 = [r1[h] + beta[h] * q[h] for h in each]
    s1, a1 = apply_matrix(p1)
    d1 = [row_dot(p1[h], a1[h]) + EPS for h in each]
    al1 = [n1[h] / d1[h] for h in each]

    al1b = [row_dot(xb[h], p1[h]) for h in each]
    n1b = [al1b[h] / d1[h] for h in each]
    d1b = [-n1b[h] * al1[h] for h in each]
    p1b = [al1[h] * xb[h] + (2.0 * d1b[h]) * a1[h] for h in each]
    betab = [row_dot(p1b[h], q[h]) for h in each]
    n1b = [n1b[h] + betab[h] / (n0[h] + EPS) for h in each]
    n0b = [-betab[h] * beta[h] / (n0[h] + EPS) for h in each]
    r1b = [p1b[h] + (2.0 * n1b[h]) * r1[h] for h in each]
    al0b = [row_dot(xb[h], q[h]) - row_dot(r1b[h], a0[h]) for h in each]
    d0b = [-al0b[h] * al0[h] / d0[h] for h in each]
    n0b = [n0b[h] + al0b[h] / d0[h] for h in each]
    a0b = [d0b[h] * q[h] - al0[h] * r1b[h] for h in each]
    s2, back = apply_matrix(a0b)

    cov_out, valkey_out = [], []
    for h in each:
        here = slice(h * size, (h + 1) * size)
        x = al0[h] * q[h] + al1[h] * p1[h]
        sx = al0[h] * s0[h] + al1[h] * s1[h]
        c1 = (2.0 * d1b[h]) * p1[h]
        gq_ref[:, here] = (
            beta[h] * p1b[h] + al0[h] * xb[h] + d0b[h] * a0[h] + back[h] + r1b[h]
            + (2.0 * n0b[h]) * q[h]
        )
        x2, q2, p2, a2, do2_right = right(x), right(q[h]), right(p1[h]), right(a0b[h]), right(do[h])
        c2 = right(c1)
        gk_ref[:, here] = (
            mul(left(sw[h].T), x2) + mul(left(s1[h].T), c2)
            + mul(left(s0[h].T), a2) + mul(left(s2[h].T), q2)
        )
        gv_ref[:, here] = mul(left(sx.T), do2_right)
        turned = mul(left(a0b[h].T), q2)
        cov_out.append(mul(left(c1.T), p2) + turned + turned.T)
        valkey_out.append(mul(left(do[h].T), x2))
    pack(cov_out, valkey_out, out_ref)


def final_kernel(
    k_ref, v_ref, gq_ref, gk_ref, gv_ref, state_ref, gq_out, gk_out, gv_out, *, heads, size
):
    gq_out[...] = gq_ref[...]
    cov, valkey = unpack(state_ref, size)
    for h in range(heads):
        here = slice(h * size, (h + 1) * size)
        k2 = left(k_ref[:, here])
        v2 = left(v_ref[:, here])
        gk_out[:, here] = gk_ref[:, here] + mul(k2, right(cov[h])) + mul(v2, right(valkey[h]))
        gv_out[:, here] = gv_ref[:, here] + mul_t(k2, right_t(valkey[h]))


VMEM = pl.BlockSpec(memory_space=pltpu.VMEM)
SMEM = pl.BlockSpec(memory_space=pltpu.SMEM)
MIB = 1024 * 1024


def call(kernel, in_specs, out_shape, limit=32):
    out_specs = VMEM if not isinstance(out_shape, tuple) else (VMEM,) * len(out_shape)
    return pl.pallas_call(
        kernel, in_specs=in_specs, out_specs=out_specs, out_shape=out_shape,
        compiler_params=pltpu.CompilerParams(vmem_limit_bytes=limit * MIB),
    )


def split_blocks(count):
    inner = 16 if count % 16 == 0 and count > 16 else max(1, count // 4)
    return inner, count // inner


def scan_over(state, backward, beside):
    inner, groups = split_blocks(lax.axis_size("seq"))
    within = [[g * inner + i for i in range(inner)] for g in range(groups)]
    across = [[g * inner + i for g in range(groups)] for i in range(inner)]

    def exchange(array, members):
        return lax.all_to_all(array, "seq", 0, 0, axis_index_groups=members, tiled=True)

    received, beside = lax.optimization_barrier((exchange(state, within), beside))
    received = received.reshape(inner, -1)
    same = jax.ShapeDtypeStruct(received.shape, F32)
    sums, totals = call(
        functools.partial(inner_kernel, backward=backward),
        [SMEM, VMEM],
        (same, jax.ShapeDtypeStruct((groups, received.shape[1]), F32)),
    )(beside[0], received)
    result = call(outer_kernel, [VMEM, VMEM], same)(sums, exchange(totals, across))
    return exchange(result, within), beside


def on_device(queries, keys, values, out_grad, w_out, ridge):
    tokens, columns = queries.shape
    heads = ridge.shape[0]
    size = columns // heads
    sizes = dict(heads=heads, size=size)
    local = jax.ShapeDtypeStruct((tokens, columns), F32)
    parts = split_blocks(lax.axis_size("seq"))[0]
    state_shape = jax.ShapeDtypeStruct((parts, (3 * size // parts + 1) * size), F32)

    states_shape = jax.ShapeDtypeStruct((parts, 1, state_shape.shape[1]), F32)
    states = call(functools.partial(state_kernel, **sizes), [VMEM] * 2, states_shape, 60)(keys, values)
    d_out = lax.dot_general(
        lax.all_gather(out_grad, "head", axis=1, tiled=True),
        w_out,
        (((1,), (1,)), ((), ())),
        preferred_element_type=F32,
    )
    group = (lax.axis_index("seq") // split_blocks(lax.axis_size("seq"))[0]).astype(jnp.int32)
    ridge_row = jnp.repeat(ridge, size)[None]
    halved = jax.ShapeDtypeStruct((heads, 2 * size, 2 * size), BF16)
    *here, value_halves = call(
        functools.partial(query_kernel, **sizes), [VMEM] * 3, (local,) * 3 + (halved,) * 3
    )(queries, keys, values)
    here += call(functools.partial(cotangent_kernel, **sizes), [VMEM] * 3, (local,) * 2)(
        d_out, here[3], value_halves
    )
    before, (group, ridge_row, d_out, *here) = scan_over(
        states, False, (group.reshape(1), ridge_row, d_out, *here)
    )
    grad_q, grad_k, grad_v, adjoints = call(
        functools.partial(main_kernel, **sizes), [VMEM] * 10, (local, local, local, state_shape)
    )(ridge_row, d_out, *here, before)
    later, _ = scan_over(adjoints, True, (group,))
    return call(functools.partial(final_kernel, **sizes), [VMEM] * 6, (local,) * 3)(
        keys, values, grad_q, grad_k, grad_v, later
    )


def solution(mesh):
    rows = P("seq", "head")
    return jax.shard_map(
        on_device,
        mesh=mesh,
        in_specs=(rows, rows, rows, rows, P("head", None), P("head")),
        out_specs=(rows, rows, rows),
        check_vma=False,
    )
```
